32 devices in a mesh: groups: 2 (over y), dp: 8 (over z, x), cuts: 2 (over core).
Axes of the slice: x: 2, y: 2, z: 4, core: 2. Of those that a mesh axis runs over, the one named last changes fastest.
Arguments:
- activations: bfloat16 [768, 7168], P(('groups', 'dp'), 'cuts'), parts along dimension 0, may hold values from -6 to 6
- out_grads: bfloat16 [768, 4096], P(('groups', 'dp'), 'cuts'), parts along dimension 0, may hold values from -6 to 6
- counts: int32 [16, 8], P(('groups', 'dp')), parts along dimension 0, may hold values from 1 to 24, 48 in all within a row
- doc_slots: int32 [128], P('groups'), parts along dimension 0, may hold values from 0 to 63, each once
- proj_in: bfloat16 [7168, 64], P('cuts'), may hold values from -0.0625 to 0.0625
- proj_out: bfloat16 [4096, 64], P('cuts'), may hold values from -0.09375 to 0.09375
- queries: bfloat16 [512, 4096], P(None, ('dp', 'cuts')), may hold values from -0.5 to 0.5
Outputs:
- scores: float32 [512, 128], P(('dp', 'cuts'), 'groups'), parts along dimension 1
The draws below stay inside these ranges and needn't reach their ends.
There are 2 independent parts, one for each index of `groups`. The reference program is written for one: setup_inputs(seed, part) draws one part's arguments, and reference() takes and returns one part's arrays. A program takes and returns all parts, laid end to end along the dimension named above; an argument that names none is the same for every part. Nothing has to cross between parts.
Inputs may be any that keep to these rules, and one draw needn't show every extreme that they name: The 8 counts of each dp index sum to 48. `doc_slots`: each document gets a different column.
All inputs are finite; a program needn't handle non-finite values.
Results may differ from the reference program's by a relative error of at most 0.0029.
Values may be sent and summed in bfloat16 or wider, within the bound.
A program may use at most 64 MiB of HBM per device.

```python
import math
import jax
import jax.numpy as jnp
import numpy as np
from jax import lax

D = 4096
FF = 7168
RANK = 64
QUERIES = 512
ROWS_DEV = 48
DOC_DEV = 8
SRC = 8
DOCS = 64
ROWS = 384
ENTRIES = 4096


def block_levels(own_key, extent, pieces, smallest, largest):
    loudness, own = 1.0, jax.random.fold_in(own_key, 6)
    for dim, shards_of in pieces:
        heights = jnp.exp(jax.random.uniform(jax.random.fold_in(own, dim), (shards_of,), jnp.float32, smallest / len(pieces), largest / len(pieces)))
        loudness = loudness * jnp.repeat(heights, extent[dim] // shards_of).reshape([-1 if axis == dim else 1 for axis in range(len(extent))])
    return loudness


def profile(amount, total, bound, skew):
    portions = [(1 << 20) // math.isqrt(rank ** skew) + 1 for rank in range(2, amount + 1)]
    surplus, given = total - bound - (amount - 1), [1] * (amount - 1)
    while surplus > 0:
        candidates = [i for i in range(amount - 1) if given[i] < bound]
        pool, left = sum([portions[i] for i in candidates]), surplus
        for i in candidates:
            addition = min(bound - given[i], max(1, left * portions[i] // pool), surplus)
            given[i] = given[i] + addition
            surplus = surplus - addition
    return np.array([bound] + given)


def ragged_sizes(rng, count, total, reach, lean):
    if count == 2:
        one = jax.random.randint(rng, (), max(1, total - reach), min(reach, total - 1) + 1)
        return jnp.stack([one, total - one])
    tallies = jnp.asarray(profile(count, total, reach, lean), jnp.int32)
    couples = (count - 1) // 2
    source_of, sink = tallies[1:1 + 2 * couples:2], tallies[2:2 + 2 * couples:2]
    slack = jnp.minimum(source_of - 1, reach - sink)
    shifted = jax.random.randint(jax.random.fold_in(rng, 1), (couples,), 0, 1 << 20) % (slack + 1)
    tallies = tallies.at[1:1 + 2 * couples:2].set(source_of - shifted).at[2:2 + 2 * couples:2].set(sink + shifted)
    return tallies[jax.random.permutation(jax.random.fold_in(rng, 2), count)]


def normal_values(rng, dims, width, bound, cuts=(), kind=jnp.bfloat16):
    result = jax.random.normal(rng, dims, jnp.float32) * width
    if len(cuts) > 0:
        result = block_levels(rng, dims, cuts, -0.22, 0.18) * result
    return jnp.clip(result, min=-bound, max=bound).astype(kind)


def setup_inputs(seed: int = 0, part: int = 0) -> dict:
    seeds = jax.random.split(jax.random.key(seed), 8)
    own_keys = jax.random.split(jax.random.fold_in(seeds[7], part), 8)
    activations = normal_values(own_keys[0], (ROWS, FF), 1.0, 6.0, ((0, 8), (1, 2)))
    out_grads = normal_values(own_keys[1], (ROWS, D), 1.0, 6.0, ((0, 8), (1, 2)))
    counts = jax.vmap(lambda own: ragged_sizes(own, DOC_DEV, ROWS_DEV, ROWS_DEV // 2, 2))(jax.random.split(own_keys[2], SRC)).reshape((SRC, DOC_DEV)).astype(jnp.int32)
    doc_slots = jax.random.permutation(own_keys[3], DOCS).astype(jnp.int32)
    proj_in = normal_values(seeds[4], (FF, RANK), FF ** -0.5, 0.0625, ((0, 2),))
    proj_out = normal_values(seeds[5], (D, RANK), D ** -0.5, 0.09375, ((0, 2),))
    queries = normal_values(seeds[6], (QUERIES, ENTRIES), 0.0625, 0.5, ((1, 16),))
    return dict(activations=activations, out_grads=out_grads, counts=counts, doc_slots=doc_slots, proj_in=proj_in, proj_out=proj_out, queries=queries)


def reference(activations, out_grads, counts, doc_slots, proj_in, proj_out, queries):
    def one_source(packed):
        acts_rows, grad_rows, doc_counts = packed
        inward = jnp.dot(acts_rows, proj_in, preferred_element_type=jnp.float32)
        outward = jnp.dot(grad_rows, proj_out, preferred_element_type=jnp.float32)
        ending = jnp.cumsum(doc_counts).astype(jnp.int32)
        position = lax.iota(jnp.int32, ROWS_DEV)
        owner_doc = jnp.sum((ending[None, :] <= position[:, None]).astype(jnp.int32), axis=1)
        member = (owner_doc[:, None] == lax.iota(jnp.int32, DOC_DEV)[None, :]).astype(jnp.float32)
        weights = member / doc_counts.astype(jnp.float32)[None, :]
        gradient = jnp.einsum("td,tr,ti->dri", weights, outward, inward, precision=lax.Precision.HIGHEST)
        return gradient.reshape(DOC_DEV, RANK * RANK)

    per_source = lax.map(one_source, (activations.reshape(SRC, ROWS_DEV, FF), out_grads.reshape(SRC, ROWS_DEV, D), counts))
    gradients = per_source.reshape(DOCS, RANK * RANK).astype(jnp.bfloat16)
    source_scores = lax.dot_general(queries, gradients, (((1,), (1,)), ((), ())), preferred_element_type=jnp.float32)
    inverse = jnp.argsort(doc_slots).astype(jnp.int32)
    return jnp.take(source_scores, inverse, axis=1)
```

```python
import functools

import jax
import jax.numpy as jnp
from jax import lax
from jax.experimental import pallas as pl
from jax.experimental.pallas import tpu as pltpu
from jax.sharding import PartitionSpec as P

LANES = 128
MESH = pl.DeviceIdType.MESH


def general(activations, out_grads, counts, doc_slots, proj_in, proj_out, queries):
    row_count = activations.shape[0]
    rank_size = proj_in.shape[1]
    doc_count = counts.shape[1]
    cut_count = lax.axis_size("cuts")
    data_count = lax.axis_size("dp")
    inward_part = jnp.dot(activations, proj_in, preferred_element_type=jnp.float32)
    outward_part = jnp.dot(out_grads, proj_out, preferred_element_type=jnp.float32)
    inward, outward = lax.psum((inward_part, outward_part), "cuts")
    earlier = lax.iota(jnp.int32, doc_count)[:, None] <= lax.iota(jnp.int32, doc_count)[None, :]
    ending = jnp.sum(jnp.where(earlier, counts[0][:, None], 0), axis=0)
    position = lax.iota(jnp.int32, row_count)
    owner_doc = jnp.sum((ending[None, :] <= position[:, None]).astype(jnp.int32), axis=1)
    member = (owner_doc[:, None] == lax.iota(jnp.int32, doc_count)[None, :]).astype(jnp.float32)
    weights = member / counts[0].astype(jnp.float32)[None, :]
    spread = (weights[:, :, None] * outward[:, None, :]).reshape(row_count, doc_count * rank_size)
    gradients = lax.dot_general(
        spread,
        inward,
        (((0,), (0,)), ((), ())),
        precision=lax.Precision.HIGHEST,
        preferred_element_type=jnp.float32,
    )
    gradients = gradients.reshape(doc_count, rank_size * rank_size).astype(jnp.bfloat16)
    slice_width = gradients.shape[1] // (cut_count * data_count)
    arranged = gradients.reshape(doc_count, data_count, cut_count, slice_width)
    picked = lax.dynamic_index_in_dim(arranged, lax.axis_index("cuts"), 2, keepdims=False).reshape(
        doc_count, data_count * slice_width
    )
    inverse = jnp.argsort(doc_slots)
    arrived = lax.all_to_all(picked, "dp", split_axis=1, concat_axis=0, tiled=True)
    ordered = jnp.take(arrived, inverse, axis=0)
    partial_value = lax.dot_general(
        queries, ordered, (((1,), (1,)), ((), ())), preferred_element_type=jnp.float32
    )
    return lax.psum_scatter(partial_value, ("dp", "cuts"), scatter_dimension=0, tiled=True)


def split(value):
    high = value.astype(jnp.bfloat16)
    return high, (value - high.astype(jnp.float32)).astype(jnp.bfloat16)


def dot(a, b):
    return jnp.dot(a, b, preferred_element_type=jnp.float32)


def dot_nt(a, b):
    return lax.dot_general(a, b, (((1,), (1,)), ((), ())), preferred_element_type=jnp.float32)


def kernel(
    n, chunks,
    counts_ref, slots_ref, act_hbm, grad_hbm, pin_hbm, pout_hbm, q_hbm, o_ref,
    act, grad, pin, pout, q, mine, other, g_send, g_recv, s_send, s_recv,
    in_sems, q_sems, pair_sems, g_send_sems, g_recv_sems, s_send_sems, s_recv_sems,
):
    me = lax.axis_index("dp")
    core = lax.axis_index("cuts")
    rows = act.shape[0]
    rank = pin.shape[0]
    docs = counts_ref.shape[1]
    groups = g_recv.shape[1] // docs
    all_docs = n * docs

    loads = []
    for a_hbm, a, p_hbm, p, count in ((act_hbm, act, pin_hbm, pin, chunks[0]), (grad_hbm, grad, pout_hbm, pout, chunks[1])):
        size = a.shape[1] // count
        for k in range(count):
            at = pl.ds(k * size, size)
            slot = len(loads)
            pair = (
                pltpu.make_async_copy(a_hbm.at[:, at], a.at[:, at], in_sems.at[2 * slot]),
                pltpu.make_async_copy(p_hbm.at[:, at], p.at[:, at], in_sems.at[2 * slot + 1]),
            )
            for copy in pair:
                copy.start()
            loads.append((pair, a, p, at))
    q_own = pltpu.make_async_copy(q_hbm.at[:, core], q.at[core], q_sems.at[0])
    q_own.start()

    barrier = pltpu.get_barrier_semaphore()
    pl.semaphore_signal(barrier, inc=1, device_id={"cuts": 1 - core}, device_id_type=MESH)
    for step in range(1, n):
        pl.semaphore_signal(barrier, inc=1, device_id={"dp": lax.rem(me + step, n)}, device_id_type=MESH)

    doc_of = lax.broadcasted_iota(jnp.int32, (docs, rows), 0)
    position = lax.broadcasted_iota(jnp.int32, (docs, rows), 1)
    first = jnp.zeros((docs, rows), jnp.int32)
    size = jnp.ones((docs, rows), jnp.int32)
    start = jnp.int32(0)
    for d in range(docs):
        here = counts_ref[0, d]
        first = jnp.where(doc_of == d, start, first)
        size = jnp.where(doc_of == d, here, size)
        start = start + here
    member = jnp.logical_and(position >= first, position < first + size)
    weights = jnp.where(member, 1.0 / size.astype(jnp.float32), 0.0)
    column = lax.broadcasted_iota(jnp.int32, (2 * all_docs, all_docs), 0)
    column = jnp.where(column >= all_docs, column - all_docs, column)
    place = jnp.where(column == slots_ref[...], 1.0, 0.0).astype(jnp.bfloat16)

    inward = jnp.zeros((rows, rank), jnp.float32)
    outward = jnp.zeros((rows, rank), jnp.float32)
    for number, (pair, a, p, at) in enumerate(loads):
        for copy in pair:
            copy.wait()
        product = dot_nt(a[:, at], p[:, at])
        if number < chunks[0]:
            inward = inward + product
        else:
            outward = outward + product
    mine[...] = jnp.concatenate([inward, outward], axis=1)

    pl.semaphore_wait(barrier, n)
    pair_copy = pltpu.make_async_remote_copy(
        src_ref=mine, dst_ref=other, send_sem=pair_sems.at[0], recv_sem=pair_sems.at[1],
        device_id={"cuts": 1 - core}, device_id_type=MESH,
    )
    pair_copy.start()
    q_pair = pltpu.make_async_remote_copy(
        src_ref=q_hbm.at[:, 1 - core], dst_ref=q.at[core], send_sem=q_sems.at[1], recv_sem=q_sems.at[2],
        device_id={"cuts": 1 - core}, device_id_type=MESH,
    )
    q_pair.start()
    pair_copy.wait_recv()
    both = mine[...] + other[...]

    low = lax.broadcasted_iota(jnp.int32, (rows, 2 * rank), 1) < rank
    turned = pltpu.roll(both, rank, 1)
    right = (jnp.where(low, both, 0.0), jnp.where(low, 0.0, turned))
    flipped = both.T
    gradients = jnp.zeros((rank // 2 * docs, 2 * rank), jnp.float32)
    for parity in range(2):
        left = jnp.concatenate(
            [flipped[rank + r:rank + r + 1, :] * weights for r in range(parity, rank, 2)], axis=0
        )
        left_high, left_low = split(left)
        right_high, right_low = split(right[parity])
        gradients = gradients + (dot(left_high, right_high) + (dot(left_high, right_low) + dot(left_low, right_high)))
    g_send[...] = gradients.astype(jnp.bfloat16).reshape(g_send.shape)

    g_copies = []
    for step in range(1, n):
        peer = lax.rem(me + step, n)
        copy = pltpu.make_async_remote_copy(
            src_ref=g_send.at[peer], dst_ref=g_recv.at[me],
            send_sem=g_send_sems.at[step], recv_sem=g_recv_sems.at[step],
            device_id={"dp": peer}, device_id_type=MESH,
        )
        copy.start()
        g_copies.append(copy)
    g_recv[me] = g_send[me]
    q_own.wait()
    q_pair.wait_recv()
    for copy in g_copies:
        copy.wait_recv()

    arrived = g_recv[...].astype(jnp.float32)
    arranged = jnp.concatenate(
        [arrived[:, m * docs:(m + 1) * docs, :].reshape(all_docs, 2 * rank) for m in range(groups)], axis=1
    ).astype(jnp.bfloat16)
    ordered = dot(place, arranged).astype(jnp.bfloat16)
    cuts, _, out_rows, width = q.shape
    scores = jnp.zeros((n * out_rows, 2 * all_docs), jnp.float32)
    for k in range(cuts):
        scores = scores + dot_nt(q[k].reshape(n * out_rows, width), ordered[:, k * width:(k + 1) * width])
    scores = scores.reshape(n, 2, out_rows // 2, 2 * all_docs)
    first_half = lax.broadcasted_iota(jnp.int32, (n, out_rows // 2, 2 * all_docs), 2) < all_docs
    s_send[...] = jnp.where(first_half, scores[:, 0], scores[:, 1])

    s_copies = []
    for step in range(1, n):
        peer = lax.rem(me + step, n)
        copy = pltpu.make_async_remote_copy(
            src_ref=s_send.at[peer], dst_ref=s_recv.at[me],
            send_sem=s_send_sems.at[step], recv_sem=s_recv_sems.at[step],
            device_id={"dp": peer}, device_id_type=MESH,
        )
        copy.start()
        s_copies.append(copy)
    s_recv[me] = s_send[me]
    for copy in s_copies:
        copy.wait_recv()
    total = s_recv[0]
    for source in range(1, n):
        total = total + s_recv[source]
    half = out_rows // 2
    o_ref[0:half, :] = total[:, :all_docs]
    o_ref[half:out_rows, :] = total[:, all_docs:]
    pair_copy.wait_send()
    q_pair.wait_send()
    for copy in g_copies + s_copies:
        copy.wait_send()


def fused(activations, out_grads, counts, doc_slots, proj_in, proj_out, queries):
    n = lax.axis_size("dp")
    cuts = lax.axis_size("cuts")
    rows, rank, docs = activations.shape[0], proj_in.shape[1], counts.shape[1]
    all_docs = n * docs
    query_count, width = queries.shape
    out_rows = query_count // (n * cuts)
    block = cuts * width // LANES * docs
    chunks = (2, 1)
    anywhere = pl.BlockSpec(memory_space=pltpu.HBM)
    bf16, f32 = jnp.bfloat16, jnp.float32
    return pl.pallas_call(
        functools.partial(kernel, n, chunks),
        out_shape=jax.ShapeDtypeStruct((out_rows, all_docs), f32),
        in_specs=[
            pl.BlockSpec(memory_space=pltpu.SMEM),
            pl.BlockSpec(memory_space=pltpu.VMEM),
            anywhere, anywhere, anywhere, anywhere, anywhere,
        ],
        out_specs=pl.BlockSpec(memory_space=pltpu.VMEM),
        scratch_shapes=[
            pltpu.VMEM(activations.shape, bf16),
            pltpu.VMEM(out_grads.shape, bf16),
            pltpu.VMEM(proj_in.shape[::-1], bf16),
            pltpu.VMEM(proj_out.shape[::-1], bf16),
            pltpu.VMEM((cuts, n, out_rows, width), bf16),
            pltpu.VMEM((rows, 2 * rank), f32),
            pltpu.VMEM((rows, 2 * rank), f32),
            pltpu.VMEM((n, block, LANES), bf16),
            pltpu.VMEM((n, block, LANES), bf16),
            pltpu.VMEM((n, out_rows // 2, 2 * all_docs), f32),
            pltpu.VMEM((n, out_rows // 2, 2 * all_docs), f32),
            pltpu.SemaphoreType.DMA((2 * sum(chunks),)),
            pltpu.SemaphoreType.DMA((3,)),
            pltpu.SemaphoreType.DMA((2,)),
            pltpu.SemaphoreType.DMA((n,)),
            pltpu.SemaphoreType.DMA((n,)),
            pltpu.SemaphoreType.DMA((n,)),
            pltpu.SemaphoreType.DMA((n,)),
        ],
        compiler_params=pltpu.CompilerParams(
            collective_id=0, has_side_effects=True, vmem_limit_bytes=48 * 1024 * 1024
        ),
    )(
        counts, doc_slots.reshape(1, all_docs), activations, out_grads, proj_in.T, proj_out.T,
        queries.reshape(n, cuts, out_rows, width),
    )


def on_device(activations, out_grads, counts, doc_slots, proj_in, proj_out, queries):
    n, cuts = lax.axis_size("dp"), lax.axis_size("cuts")
    rank, docs = proj_in.shape[1], counts.shape[1]
    width = queries.shape[1]
    fits = (
        cuts == 2
        and 2 * rank == LANES
        and width % LANES == 0
        and docs % 8 == 0
        and (cuts * width // LANES * docs) % 16 == 0
        and 2 * n * docs == LANES
        and queries.shape[0] % (n * cuts * 16) == 0
        and activations.shape[0] % 16 == 0
    )
    body = fused if fits else general
    return body(activations, out_grads, counts, doc_slots, proj_in, proj_out, queries)


def solution(mesh):
    placed = (
        P(("groups", "dp"), "cuts"),
        P(("groups", "dp"), "cuts"),
        P(("groups", "dp"), None),
        P("groups"),
        P("cuts", None),
        P("cuts", None),
        P(None, ("dp", "cuts")),
    )
    return jax.shard_map(
        on_device,
        mesh=mesh,
        in_specs=placed,
        out_specs=P(("dp", "cuts"), "groups"),
        check_vma=False,
    )
```

```python
import functools

import jax
import jax.numpy as jnp
from jax import lax
from jax.experimental import pallas as pl
from jax.experimental.pallas import tpu as pltpu
from jax.sharding import PartitionSpec as P

LANES = 128
MESH = pl.DeviceIdType.MESH


def general(activations, out_grads, counts, doc_slots, proj_in, proj_out, queries):
    row_count = activations.shape[0]
    rank_size = proj_in.shape[1]
    doc_count = counts.shape[1]
    cut_count = lax.axis_size("cuts")
    data_count = lax.axis_size("dp")
    inward_part = jnp.dot(activations, proj_in, preferred_element_type=jnp.float32)
    outward_part = jnp.dot(out_grads, proj_out, preferred_element_type=jnp.float32)
    inward, outward = lax.psum((inward_part, outward_part), "cuts")
    earlier = lax.iota(jnp.int32, doc_count)[:, None] <= lax.iota(jnp.int32, doc_count)[None, :]
    ending = jnp.sum(jnp.where(earlier, counts[0][:, None], 0), axis=0)
    position = lax.iota(jnp.int32, row_count)
    owner_doc = jnp.sum((ending[None, :] <= position[:, None]).astype(jnp.int32), axis=1)
    member = (owner_doc[:, None] == lax.iota(jnp.int32, doc_count)[None, :]).astype(jnp.float32)
    weights = member / counts[0].astype(jnp.float32)[None, :]
    spread = (weights[:, :, None] * outward[:, None, :]).reshape(row_count, doc_count * rank_size)
    gradients = lax.dot_general(
        spread,
        inward,
        (((0,), (0,)), ((), ())),
        precision=lax.Precision.HIGHEST,
        preferred_element_type=jnp.float32,
    )
    gradients = gradients.reshape(doc_count, rank_size * rank_size).astype(jnp.bfloat16)
    slice_width = gradients.shape[1] // (cut_count * data_count)
    arranged = gradients.reshape(doc_count, data_count, cut_count, slice_width)
    picked = lax.dynamic_index_in_dim(arranged, lax.axis_index("cuts"), 2, keepdims=False).reshape(
        doc_count, data_count * slice_width
    )
    inverse = jnp.argsort(doc_slots)
    arrived = lax.all_to_all(picked, "dp", split_axis=1, concat_axis=0, tiled=True)
    ordered = jnp.take(arrived, inverse, axis=0)
    partial_value = lax.dot_general(
        queries, ordered, (((1,), (1,)), ((), ())), preferred_element_type=jnp.float32
    )
    return lax.psum_scatter(partial_value, ("dp", "cuts"), scatter_dimension=0, tiled=True)


def split(value):
    high = value.astype(jnp.bfloat16)
    return high, (value - high.astype(jnp.float32)).astype(jnp.bfloat16)


def dot(a, b):
    return jnp.dot(a, b, preferred_element_type=jnp.float32)


def dot_nt(a, b):
    return lax.dot_general(a, b, (((1,), (1,)), ((), ())), preferred_element_type=jnp.float32)


def kernel(
    n, chunks,
    counts_ref, slots_ref, act_hbm, grad_hbm, pin_hbm, pout_hbm, q_hbm, o_ref,
    act, grad, pin, pout, q, mine, other, g_send, g_recv, s_send, s_recv,
    in_sems, q_sems, pair_sems, g_send_sems, g_recv_sems, s_send_sems, s_recv_sems,
):
    me = lax.axis_index("dp")
    core = lax.axis_index("cuts")
    rows = act.shape[0]
    rank = pin.shape[0]
    docs = counts_ref.shape[1]
    groups = g_recv.shape[1] // docs
    all_docs = n * docs

    loads = []
    for a_hbm, a, p_hbm, p, count in ((act_hbm, act, pin_hbm, pin, chunks[0]), (grad_hbm, grad, pout_hbm, pout, chunks[1])):
        size = a.shape[1] // count
        for k in range(count):
            at = pl.ds(k * size, size)
            slot = len(loads)
            pair = (
                pltpu.make_async_copy(a_hbm.at[:, at], a.at[:, at], in_sems.at[2 * slot]),
                pltpu.make_async_copy(p_hbm.at[:, at], p.at[:, at], in_sems.at[2 * slot + 1]),
            )
            for copy in pair:
                copy.start()
            loads.append((pair, a, p, at))
    q_own = pltpu.make_async_copy(q_hbm.at[:, core], q.at[core], q_sems.at[0])
    q_own.start()

    barrier = pltpu.get_barrier_semaphore()
    pl.semaphore_signal(barrier, inc=1, device_id={"cuts": 1 - core}, device_id_type=MESH)
    for step in range(1, n):
        pl.semaphore_signal(barrier, inc=1, device_id={"dp": lax.rem(me + step, n)}, device_id_type=MESH)

    doc_of = lax.broadcasted_iota(jnp.int32, (docs, rows), 0)
    position = lax.broadcasted_iota(jnp.int32, (docs, rows), 1)
    first = jnp.zeros((docs, rows), jnp.int32)
    size = jnp.ones((docs, rows), jnp.int32)
    start = jnp.int32(0)
    for d in range(docs):
        here = counts_ref[0, d]
        first = jnp.where(doc_of == d, start, first)
        size = jnp.where(doc_of == d, here, size)
        start = start + here
    member = jnp.logical_and(position >= first, position < first + size)
    weights = jnp.where(member, 1.0 / size.astype(jnp.float32), 0.0)
    column = lax.broadcasted_iota(jnp.int32, (2 * all_docs, all_docs), 0)
    column = jnp.where(column >= all_docs, column - all_docs, column)
    place = jnp.where(column == slots_ref[...], 1.0, 0.0).astype(jnp.bfloat16)

    inward = jnp.zeros((rows, rank), jnp.float32)
    outward = jnp.zeros((rows, rank), jnp.float32)
    for number, (pair, a, p, at) in enumerate(loads):
        for copy in pair:
            copy.wait()
        product = dot_nt(a[:, at], p[:, at])
        if number < chunks[0]:
            inward = inward + product
        else:
            outward = outward + product
    mine[...] = jnp.concatenate([inward, outward], axis=1)

    pl.semaphore_wait(barrier, n)
    pair_copy = pltpu.make_async_remote_copy(
        src_ref=mine, dst_ref=other, send_sem=pair_sems.at[0], recv_sem=pair_sems.at[1],
        device_id={"cuts": 1 - core}, device_id_type=MESH,
    )
    pair_copy.start()
    q_pair = pltpu.make_async_remote_copy(
        src_ref=q_hbm.at[:, 1 - core], dst_ref=q.at[core], send_sem=q_sems.at[1], recv_sem=q_sems.at[2],
        device_id={"cuts": 1 - core}, device_id_type=MESH,
    )
    q_pair.start()
    pair_copy.wait_recv()
    both = mine[...] + other[...]

    low = lax.broadcasted_iota(jnp.int32, (rows, 2 * rank), 1) < rank
    turned = pltpu.roll(both, rank, 1)
    right = (jnp.where(low, both, 0.0), jnp.where(low, 0.0, turned))
    flipped = both.T
    gradients = jnp.zeros((rank // 2 * docs, 2 * rank), jnp.float32)
    for parity in range(2):
        left = jnp.concatenate(
            [flipped[rank + r:rank + r + 1, :] * weights for r in range(parity, rank, 2)], axis=0
        )
        left_high, left_low = split(left)
        right_high, right_low = split(right[parity])
        gradients = gradients + (dot(left_high, right_high) + (dot(left_high, right_low) + dot(left_low, right_high)))
    g_send[...] = gradients.astype(jnp.bfloat16).reshape(g_send.shape)

    g_copies = []
    for step in range(1, n):
        peer = lax.rem(me + step, n)
        copy = pltpu.make_async_remote_copy(
            src_ref=g_send.at[peer], dst_ref=g_recv.at[me],
            send_sem=g_send_sems.at[step], recv_sem=g_recv_sems.at[step],
            device_id={"dp": peer}, device_id_type=MESH,
        )
        copy.start()
        g_copies.append(copy)
    g_recv[me] = g_send[me]
    q_own.wait()
    q_pair.wait_recv()
    for copy in g_copies:
        copy.wait_recv()

    arrived = g_recv[...].astype(jnp.float32)
    arranged = jnp.concatenate(
        [arrived[:, m * docs:(m + 1) * docs, :].reshape(all_docs, 2 * rank) for m in range(groups)], axis=1
    ).astype(jnp.bfloat16)
    ordered = dot(place, arranged).astype(jnp.bfloat16)
    cuts, _, out_rows, width = q.shape
    scores = jnp.zeros((n * out_rows, 2 * all_docs), jnp.float32)
    for k in range(cuts):
        scores = scores + dot_nt(q[k].reshape(n * out_rows, width), ordered[:, k * width:(k + 1) * width])
    scores = scores.reshape(n, 2, out_rows // 2, 2 * all_docs)
    first_half = lax.broadcasted_iota(jnp.int32, (n, out_rows // 2, 2 * all_docs), 2) < all_docs
    s_send[...] = jnp.where(first_half, scores[:, 0], scores[:, 1])

    s_copies = []
    for step in range(1, n):
        peer = lax.rem(me + step, n)
        copy = pltpu.make_async_remote_copy(
            src_ref=s_send.at[peer], dst_ref=s_recv.at[me],
            send_sem=s_send_sems.at[step], recv_sem=s_recv_sems.at[step],
            device_id={"dp": peer}, device_id_type=MESH,
        )
        copy.start()
        s_copies.append(copy)
    s_recv[me] = s_send[me]
    for copy in s_copies:
        copy.wait_recv()
    total = s_recv[0]
    for source in range(1, n):
        total = total + s_recv[source]
    half = out_rows // 2
    o_ref[0:half, :] = total[:, :all_docs]
    o_ref[half:out_rows, :] = total[:, all_docs:]
    pair_copy.wait_send()
    q_pair.wait_send()
    for copy in g_copies + s_copies:
        copy.wait_send()


def fused(activations, out_grads, counts, doc_slots, proj_in, proj_out, queries):
    n = lax.axis_size("dp")
    cuts = lax.axis_size("cuts")
    rows, rank, docs = activations.shape[0], proj_in.shape[1], counts.shape[1]
    all_docs = n * docs
    query_count, width = queries.shape
    out_rows = query_count // (n * cuts)
    block = cuts * width // LANES * docs
    chunks = (2, 1)
    anywhere = pl.BlockSpec(memory_space=pltpu.HBM)
    bf16, f32 = jnp.bfloat16, jnp.float32
    return pl.pallas_call(
        functools.partial(kernel, n, chunks),
        out_shape=jax.ShapeDtypeStruct((out_rows, all_docs), f32),
        in_specs=[
            pl.BlockSpec(memory_space=pltpu.SMEM),
            pl.BlockSpec(memory_space=pltpu.VMEM),
            anywhere, anywhere, anywhere, anywhere, anywhere,
        ],
        out_specs=pl.BlockSpec(memory_space=pltpu.VMEM),
        scratch_shapes=[
            pltpu.VMEM(activations.shape, bf16),
            pltpu.VMEM(out_grads.shape, bf16),
            pltpu.VMEM(proj_in.shape[::-1], bf16),
            pltpu.VMEM(proj_out.shape[::-1], bf16),
            pltpu.VMEM((cuts, n, out_rows, width), bf16),
            pltpu.VMEM((rows, 2 * rank), f32),
            pltpu.VMEM((rows, 2 * rank), f32),
            pltpu.VMEM((n, block, LANES), bf16),
            pltpu.VMEM((n, block, LANES), bf16),
            pltpu.VMEM((n, out_rows // 2, 2 * all_docs), f32),
            pltpu.VMEM((n, out_rows // 2, 2 * all_docs), f32),
            pltpu.SemaphoreType.DMA((2 * sum(chunks),)),
            pltpu.SemaphoreType.DMA((3,)),
            pltpu.SemaphoreType.DMA((2,)),
            pltpu.SemaphoreType.DMA((n,)),
            pltpu.SemaphoreType.DMA((n,)),
            pltpu.SemaphoreType.DMA((n,)),
            pltpu.SemaphoreType.DMA((n,)),
        ],
        compiler_params=pltpu.CompilerParams(
            collective_id=0, has_side_effects=True, vmem_limit_bytes=60 * 1024 * 1024
        ),
    )(
        counts, doc_slots.reshape(1, all_docs), activations, out_grads, proj_in.T, proj_out.T,
        queries.reshape(n, cuts, out_rows, width),
    )


def on_device(activations, out_grads, counts, doc_slots, proj_in, proj_out, queries):
    n, cuts = lax.axis_size("dp"), lax.axis_size("cuts")
    rank, docs = proj_in.shape[1], counts.shape[1]
    width = queries.shape[1]
    fits = (
        cuts == 2
        and 2 * rank == LANES
        and width % LANES == 0
        and docs % 8 == 0
        and (cuts * width // LANES * docs) % 16 == 0
        and 2 * n * docs == LANES
        and queries.shape[0] % (n * cuts * 16) == 0
        and activations.shape[0] % 16 == 0
    )
    body = fused if fits else general
    return body(activations, out_grads, counts, doc_slots, proj_in, proj_out, queries)


def solution(mesh):
    placed = (
        P(("groups", "dp"), "cuts"),
        P(("groups", "dp"), "cuts"),
        P(("groups", "dp"), None),
        P("groups"),
        P("cuts", None),
        P("cuts", None),
        P(None, ("dp", "cuts")),
    )
    return jax.shard_map(
        on_device,
        mesh=mesh,
        in_specs=placed,
        out_specs=P(("dp", "cuts"), "groups"),
        check_vma=False,
    )
```

```python
import functools

import jax
import jax.numpy as jnp
from jax import lax
from jax.experimental import pallas as pl
from jax.experimental.pallas import tpu as pltpu
from jax.sharding import PartitionSpec as P

LANES = 128
MESH = pl.DeviceIdType.MESH


def general(activations, out_grads, counts, doc_slots, proj_in, proj_out, queries):
    row_count = activations.shape[0]
    rank_size = proj_in.shape[1]
    doc_count = counts.shape[1]
    cut_count = lax.axis_size("cuts")
    data_count = lax.axis_size("dp")
    inward_part = jnp.dot(activations, proj_in, preferred_element_type=jnp.float32)
    outward_part = jnp.dot(out_grads, proj_out, preferred_element_type=jnp.float32)
    inward, outward = lax.psum((inward_part, outward_part), "cuts")
    earlier = lax.iota(jnp.int32, doc_count)[:, None] <= lax.iota(jnp.int32, doc_count)[None, :]
    ending = jnp.sum(jnp.where(earlier, counts[0][:, None], 0), axis=0)
    position = lax.iota(jnp.int32, row_count)
    owner_doc = jnp.sum((ending[None, :] <= position[:, None]).astype(jnp.int32), axis=1)
    member = (owner_doc[:, None] == lax.iota(jnp.int32, doc_count)[None, :]).astype(jnp.float32)
    weights = member / counts[0].astype(jnp.float32)[None, :]
    spread = (weights[:, :, None] * outward[:, None, :]).reshape(row_count, doc_count * rank_size)
    gradients = lax.dot_general(
        spread,
        inward,
        (((0,), (0,)), ((), ())),
        precision=lax.Precision.HIGHEST,
        preferred_element_type=jnp.float32,
    )
    gradients = gradients.reshape(doc_count, rank_size * rank_size).astype(jnp.bfloat16)
    slice_width = gradients.shape[1] // (cut_count * data_count)
    arranged = gradients.reshape(doc_count, data_count, cut_count, slice_width)
    picked = lax.dynamic_index_in_dim(arranged, lax.axis_index("cuts"), 2, keepdims=False).reshape(
        doc_count, data_count * slice_width
    )
    inverse = jnp.argsort(doc_slots)
    arrived = lax.all_to_all(picked, "dp", split_axis=1, concat_axis=0, tiled=True)
    ordered = jnp.take(arrived, inverse, axis=0)
    partial_value = lax.dot_general(
        queries, ordered, (((1,), (1,)), ((), ())), preferred_element_type=jnp.float32
    )
    return lax.psum_scatter(partial_value, ("dp", "cuts"), scatter_dimension=0, tiled=True)


def split(value):
    high = value.astype(jnp.bfloat16)
    return high, (value - high.astype(jnp.float32)).astype(jnp.bfloat16)


def dot(a, b):
    return jnp.dot(a, b, preferred_element_type=jnp.float32)


def dot_nt(a, b):
    return lax.dot_general(a, b, (((1,), (1,)), ((), ())), preferred_element_type=jnp.float32)


def kernel(
    n, chunks,
    counts_hbm, slots_hbm, act_hbm, grad_hbm, pin_hbm, pout_hbm, q_hbm, o_ref,
    counts_ref, slots_ref, act, grad, pin, pout, q, mine, other, g_send, g_recv, s_send, s_recv,
    small_sems, in_sems, q_sems, pair_sems, g_send_sems, g_recv_sems, s_send_sems, s_recv_sems,
):
    me = lax.axis_index("dp")
    core = lax.axis_index("cuts")
    rows = act.shape[0]
    rank = pin.shape[0]
    docs = counts_ref.shape[1]
    groups = g_recv.shape[1] // docs
    all_docs = n * docs

    barrier = pltpu.get_barrier_semaphore()
    pl.semaphore_signal(barrier, inc=1, device_id={"cuts": 1 - core}, device_id_type=MESH)
    for step in range(1, n):
        pl.semaphore_signal(barrier, inc=1, device_id={"dp": lax.rem(me + step, n)}, device_id_type=MESH)

    loads = []
    for a_hbm, a, p_hbm, p, count in ((act_hbm, act, pin_hbm, pin, chunks[0]), (grad_hbm, grad, pout_hbm, pout, chunks[1])):
        size = a.shape[1] // count
        for k in range(count):
            at = pl.ds(k * size, size)
            slot = len(loads)
            pair = (
                pltpu.make_async_copy(a_hbm.at[:, at], a.at[:, at], in_sems.at[2 * slot]),
                pltpu.make_async_copy(p_hbm.at[:, at], p.at[:, at], in_sems.at[2 * slot + 1]),
            )
            for copy in pair:
                copy.start()
            loads.append((pair, a, p, at))
    small = (
        pltpu.make_async_copy(counts_hbm, counts_ref, small_sems.at[0]),
        pltpu.make_async_copy(slots_hbm, slots_ref, small_sems.at[1]),
    )
    for copy in small:
        copy.start()
    q_own = pltpu.make_async_copy(q_hbm.at[:, core], q.at[core], q_sems.at[0])
    q_own.start()

    inward = jnp.zeros((rows, rank), jnp.float32)
    outward = jnp.zeros((rows, rank), jnp.float32)
    for number, (pair, a, p, at) in enumerate(loads):
        for copy in pair:
            copy.wait()
        product = dot_nt(a[:, at], p[:, at])
        if number < chunks[0]:
            inward = inward + product
        else:
            outward = outward + product
    mine[...] = jnp.concatenate([inward, outward], axis=1)

    pl.semaphore_wait(barrier, n)
    pair_copy = pltpu.make_async_remote_copy(
        src_ref=mine, dst_ref=other, send_sem=pair_sems.at[0], recv_sem=pair_sems.at[1],
        device_id={"cuts": 1 - core}, device_id_type=MESH,
    )
    pair_copy.start()
    q_pair = pltpu.make_async_remote_copy(
        src_ref=q_hbm.at[:, 1 - core], dst_ref=q.at[core], send_sem=q_sems.at[1], recv_sem=q_sems.at[2],
        device_id={"cuts": 1 - core}, device_id_type=MESH,
    )
    q_pair.start()
    for copy in small:
        copy.wait()
    doc_of = lax.broadcasted_iota(jnp.int32, (docs, rows), 0)
    position = lax.broadcasted_iota(jnp.int32, (docs, rows), 1)
    first = jnp.zeros((docs, rows), jnp.int32)
    size = jnp.ones((docs, rows), jnp.int32)
    start = jnp.int32(0)
    for d in range(docs):
        here = counts_ref[0, d]
        first = jnp.where(doc_of == d, start, first)
        size = jnp.where(doc_of == d, here, size)
        start = start + here
    member = jnp.logical_and(position >= first, position < first + size)
    weights = jnp.where(member, 1.0 / size.astype(jnp.float32), 0.0)
    column = lax.broadcasted_iota(jnp.int32, (2 * all_docs, all_docs), 0)
    column = jnp.where(column >= all_docs, column - all_docs, column)
    place = jnp.where(column == slots_ref[...], 1.0, 0.0).astype(jnp.bfloat16)

    pair_copy.wait_recv()
    both = mine[...] + other[...]

    low = lax.broadcasted_iota(jnp.int32, (rows, 2 * rank), 1) < rank
    turned = pltpu.roll(both, rank, 1)
    right = (jnp.where(low, both, 0.0), jnp.where(low, 0.0, turned))
    flipped = both.T
    gradients = jnp.zeros((rank // 2 * docs, 2 * rank), jnp.float32)
    for parity in range(2):
        left = jnp.concatenate(
            [flipped[rank + r:rank + r + 1, :] * weights for r in range(parity, rank, 2)], axis=0
        )
        left_high, left_low = split(left)
        right_high, right_low = split(right[parity])
        gradients = gradients + (dot(left_high, right_high) + (dot(left_high, right_low) + dot(left_low, right_high)))
    g_send[...] = gradients.astype(jnp.bfloat16).reshape(g_send.shape)

    g_copies = []
    for step in range(1, n):
        peer = lax.rem(me + step, n)
        copy = pltpu.make_async_remote_copy(
            src_ref=g_send.at[peer], dst_ref=g_recv.at[me],
            send_sem=g_send_sems.at[step], recv_sem=g_recv_sems.at[step],
            device_id={"dp": peer}, device_id_type=MESH,
        )
        copy.start()
        g_copies.append(copy)
    g_recv[me] = g_send[me]
    q_own.wait()
    q_pair.wait_recv()
    for copy in g_copies:
        copy.wait_recv()

    arrived = g_recv[...].astype(jnp.float32)
    arranged = jnp.concatenate(
        [arrived[:, m * docs:(m + 1) * docs, :].reshape(all_docs, 2 * rank) for m in range(groups)], axis=1
    ).astype(jnp.bfloat16)
    ordered = dot(place, arranged).astype(jnp.bfloat16)
    cuts, _, out_rows, width = q.shape
    scores = jnp.zeros((n * out_rows, 2 * all_docs), jnp.float32)
    for k in range(cuts):
        scores = scores + dot_nt(q[k].reshape(n * out_rows, width), ordered[:, k * width:(k + 1) * width])
    scores = scores.reshape(n, 2, out_rows // 2, 2 * all_docs)
    first_half = lax.broadcasted_iota(jnp.int32, (n, out_rows // 2, 2 * all_docs), 2) < all_docs
    s_send[...] = jnp.where(first_half, scores[:, 0], scores[:, 1])

    s_copies = []
    for step in range(1, n):
        peer = lax.rem(me + step, n)
        copy = pltpu.make_async_remote_copy(
            src_ref=s_send.at[peer], dst_ref=s_recv.at[me],
            send_sem=s_send_sems.at[step], recv_sem=s_recv_sems.at[step],
            device_id={"dp": peer}, device_id_type=MESH,
        )
        copy.start()
        s_copies.append(copy)
    s_recv[me] = s_send[me]
    for copy in s_copies:
        copy.wait_recv()
    total = s_recv[0]
    for source in range(1, n):
        total = total + s_recv[source]
    half = out_rows // 2
    o_ref[0:half, :] = total[:, :all_docs]
    o_ref[half:out_rows, :] = total[:, all_docs:]
    pair_copy.wait_send()
    q_pair.wait_send()
    for copy in g_copies + s_copies:
        copy.wait_send()


def fused(activations, out_grads, counts, doc_slots, proj_in, proj_out, queries):
    n = lax.axis_size("dp")
    cuts = lax.axis_size("cuts")
    rows, rank, docs = activations.shape[0], proj_in.shape[1], counts.shape[1]
    all_docs = n * docs
    query_count, width = queries.shape
    out_rows = query_count // (n * cuts)
    block = cuts * width // LANES * docs
    chunks = (2, 1)
    anywhere = pl.BlockSpec(memory_space=pltpu.HBM)
    bf16, f32 = jnp.bfloat16, jnp.float32
    return pl.pallas_call(
        functools.partial(kernel, n, chunks),
        out_shape=pltpu.VMEM((out_rows, all_docs), f32),
        in_specs=[
            anywhere, anywhere, anywhere, anywhere, anywhere, anywhere, anywhere,
        ],
        out_specs=pl.BlockSpec(memory_space=pltpu.VMEM),
        scratch_shapes=[
            pltpu.SMEM((1, docs), jnp.int32),
            pltpu.VMEM((1, all_docs), jnp.int32),
            pltpu.VMEM(activations.shape, bf16),
            pltpu.VMEM(out_grads.shape, bf16),
            pltpu.VMEM(proj_in.shape[::-1], bf16),
            pltpu.VMEM(proj_out.shape[::-1], bf16),
            pltpu.VMEM((cuts, n, out_rows, width), bf16),
            pltpu.VMEM((rows, 2 * rank), f32),
            pltpu.VMEM((rows, 2 * rank), f32),
            pltpu.VMEM((n, block, LANES), bf16),
            pltpu.VMEM((n, block, LANES), bf16),
            pltpu.VMEM((n, out_rows // 2, 2 * all_docs), f32),
            pltpu.VMEM((n, out_rows // 2, 2 * all_docs), f32),
            pltpu.SemaphoreType.DMA((2,)),
            pltpu.SemaphoreType.DMA((2 * sum(chunks),)),
            pltpu.SemaphoreType.DMA((3,)),
            pltpu.SemaphoreType.DMA((2,)),
            pltpu.SemaphoreType.DMA((n,)),
            pltpu.SemaphoreType.DMA((n,)),
            pltpu.SemaphoreType.DMA((n,)),
            pltpu.SemaphoreType.DMA((n,)),
        ],
        compiler_params=pltpu.CompilerParams(
            collective_id=0, has_side_effects=True, vmem_limit_bytes=60 * 1024 * 1024
        ),
    )(
        counts, doc_slots.reshape(1, all_docs), activations, out_grads, proj_in.T, proj_out.T,
        queries.reshape(n, cuts, out_rows, width),
    )


def on_device(activations, out_grads, counts, doc_slots, proj_in, proj_out, queries):
    n, cuts = lax.axis_size("dp"), lax.axis_size("cuts")
    rank, docs = proj_in.shape[1], counts.shape[1]
    width = queries.shape[1]
    fits = (
        cuts == 2
        and 2 * rank == LANES
        and width % LANES == 0
        and docs % 8 == 0
        and (cuts * width // LANES * docs) % 16 == 0
        and 2 * n * docs == LANES
        and queries.shape[0] % (n * cuts * 16) == 0
        and activations.shape[0] % 16 == 0
    )
    body = fused if fits else general
    return body(activations, out_grads, counts, doc_slots, proj_in, proj_out, queries)


def solution(mesh):
    placed = (
        P(("groups", "dp"), "cuts"),
        P(("groups", "dp"), "cuts"),
        P(("groups", "dp"), None),
        P("groups"),
        P("cuts", None),
        P("cuts", None),
        P(None, ("dp", "cuts")),
    )
    return jax.shard_map(
        on_device,
        mesh=mesh,
        in_specs=placed,
        out_specs=P(("dp", "cuts"), "groups"),
        check_vma=False,
    )
```

```python
import functools

import jax
import jax.numpy as jnp
from jax import lax
from jax.experimental import pallas as pl
from jax.experimental.pallas import tpu as pltpu
from jax.sharding import PartitionSpec as P

LANES = 128
MESH = pl.DeviceIdType.MESH


def general(activations, out_grads, counts, doc_slots, proj_in, proj_out, queries):
    row_count = activations.shape[0]
    rank_size = proj_in.shape[1]
    doc_count = counts.shape[1]
    cut_count = lax.axis_size("cuts")
    data_count = lax.axis_size("dp")
    inward_part = jnp.dot(activations, proj_in, preferred_element_type=jnp.float32)
    outward_part = jnp.dot(out_grads, proj_out, preferred_element_type=jnp.float32)
    inward, outward = lax.psum((inward_part, outward_part), "cuts")
    earlier = lax.iota(jnp.int32, doc_count)[:, None] <= lax.iota(jnp.int32, doc_count)[None, :]
    ending = jnp.sum(jnp.where(earlier, counts[0][:, None], 0), axis=0)
    position = lax.iota(jnp.int32, row_count)
    owner_doc = jnp.sum((ending[None, :] <= position[:, None]).astype(jnp.int32), axis=1)
    member = (owner_doc[:, None] == lax.iota(jnp.int32, doc_count)[None, :]).astype(jnp.float32)
    weights = member / counts[0].astype(jnp.float32)[None, :]
    spread = (weights[:, :, None] * outward[:, None, :]).reshape(row_count, doc_count * rank_size)
    gradients = lax.dot_general(
        spread,
        inward,
        (((0,), (0,)), ((), ())),
        precision=lax.Precision.HIGHEST,
        preferred_element_type=jnp.float32,
    )
    gradients = gradients.reshape(doc_count, rank_size * rank_size).astype(jnp.bfloat16)
    slice_width = gradients.shape[1] // (cut_count * data_count)
    arranged = gradients.reshape(doc_count, data_count, cut_count, slice_width)
    picked = lax.dynamic_index_in_dim(arranged, lax.axis_index("cuts"), 2, keepdims=False).reshape(
        doc_count, data_count * slice_width
    )
    inverse = jnp.argsort(doc_slots)
    arrived = lax.all_to_all(picked, "dp", split_axis=1, concat_axis=0, tiled=True)
    ordered = jnp.take(arrived, inverse, axis=0)
    partial_value = lax.dot_general(
        queries, ordered, (((1,), (1,)), ((), ())), preferred_element_type=jnp.float32
    )
    return lax.psum_scatter(partial_value, ("dp", "cuts"), scatter_dimension=0, tiled=True)


def split(value):
    high = value.astype(jnp.bfloat16)
    return high, (value - high.astype(jnp.float32)).astype(jnp.bfloat16)


def dot(a, b):
    return jnp.dot(a, b, preferred_element_type=jnp.float32)


def dot_nt(a, b):
    return lax.dot_general(a, b, (((1,), (1,)), ((), ())), preferred_element_type=jnp.float32)


def kernel(
    n, chunks,
    counts_hbm, slots_hbm, act_hbm, grad_hbm, pin_hbm, pout_hbm, q_hbm, o_ref,
    counts_ref, slots_ref, act, grad, pin, pout, q, mine, other, g_send, g_recv, s_send, s_recv,
    small_sems, in_sems, q_sems, pair_sems, g_send_sems, g_recv_sems, s_send_sems, s_recv_sems,
):
    me = lax.axis_index("dp")
    core = lax.axis_index("cuts")
    rows = act.shape[0]
    rank = pin.shape[0]
    docs = counts_ref.shape[1]
    groups = g_recv.shape[1] // docs
    all_docs = n * docs

    barrier = pltpu.get_barrier_semaphore()
    pl.semaphore_signal(barrier, inc=1, device_id={"cuts": 1 - core}, device_id_type=MESH)
    for step in range(1, n):
        pl.semaphore_signal(barrier, inc=1, device_id={"dp": lax.rem(me + step, n)}, device_id_type=MESH)

    loads = []
    for a_hbm, a, p_hbm, p, count in ((act_hbm, act, pin_hbm, pin, chunks[0]), (grad_hbm, grad, pout_hbm, pout, chunks[1])):
        size = a.shape[1] // count
        for k in range(count):
            at = pl.ds(k * size, size)
            slot = len(loads)
            pair = (
                pltpu.make_async_copy(a_hbm.at[:, at], a.at[:, at], in_sems.at[2 * slot]),
                pltpu.make_async_copy(p_hbm.at[:, at], p.at[:, at], in_sems.at[2 * slot + 1]),
            )
            for copy in pair:
                copy.start()
            loads.append((pair, a, p, at))
    small = (
        pltpu.make_async_copy(counts_hbm, counts_ref, small_sems.at[0]),
        pltpu.make_async_copy(slots_hbm, slots_ref, small_sems.at[1]),
    )
    for copy in small:
        copy.start()
    q_own = pltpu.make_async_copy(q_hbm.at[:, core], q.at[core], q_sems.at[0])
    q_own.start()

    inward = jnp.zeros((rows, rank), jnp.float32)
    outward = jnp.zeros((rows, rank), jnp.float32)
    for number, (pair, a, p, at) in enumerate(loads):
        for copy in pair:
            copy.wait()
        product = dot_nt(a[:, at], p[:, at])
        if number < chunks[0]:
            inward = inward + product
        else:
            outward = outward + product
    mine[...] = jnp.concatenate([inward, outward], axis=1)

    pl.semaphore_wait(barrier, n)
    pair_copy = pltpu.make_async_remote_copy(
        src_ref=mine, dst_ref=other, send_sem=pair_sems.at[0], recv_sem=pair_sems.at[1],
        device_id={"cuts": 1 - core}, device_id_type=MESH,
    )
    pair_copy.start()
    q_pair = pltpu.make_async_remote_copy(
        src_ref=q_hbm.at[:, 1 - core], dst_ref=q.at[core], send_sem=q_sems.at[1], recv_sem=q_sems.at[2],
        device_id={"cuts": 1 - core}, device_id_type=MESH,
    )
    q_pair.start()
    for copy in small:
        copy.wait()
    doc_of = lax.broadcasted_iota(jnp.int32, (docs, rows), 0)
    position = lax.broadcasted_iota(jnp.int32, (docs, rows), 1)
    first = jnp.zeros((docs, rows), jnp.int32)
    size = jnp.ones((docs, rows), jnp.int32)
    start = jnp.int32(0)
    for d in range(docs):
        here = counts_ref[0, d]
        first = jnp.where(doc_of == d, start, first)
        size = jnp.where(doc_of == d, here, size)
        start = start + here
    member = jnp.logical_and(position >= first, position < first + size)
    weights = jnp.where(member, 1.0 / size.astype(jnp.float32), 0.0)
    column = lax.broadcasted_iota(jnp.int32, (2 * all_docs, all_docs), 0)
    column = jnp.where(column >= all_docs, column - all_docs, column)
    place = jnp.where(column == slots_ref[...], 1.0, 0.0).astype(jnp.bfloat16)

    pair_copy.wait_recv()
    both = mine[...] + other[...]

    low = lax.broadcasted_iota(jnp.int32, (rows, 2 * rank), 1) < rank
    turned = pltpu.roll(both, rank, 1)
    right = (jnp.where(low, both, 0.0), jnp.where(low, 0.0, turned))
    flipped = both.T
    gradients = jnp.zeros((rank // 2 * docs, 2 * rank), jnp.float32)
    for parity in range(2):
        left = jnp.concatenate(
            [flipped[rank + r:rank + r + 1, :] * weights for r in range(parity, rank, 2)], axis=0
        )
        left_high, left_low = split(left)
        right_high, right_low = split(right[parity])
        gradients = gradients + (dot(left_high, right_high) + (dot(left_high, right_low) + dot(left_low, right_high)))
    g_send[...] = gradients.astype(jnp.bfloat16).reshape(g_send.shape)

    g_copies = []
    for step in sorted(range(1, n), key=lambda s: -abs(2 * s - n)):
        peer = lax.rem(me + step, n)
        copy = pltpu.make_async_remote_copy(
            src_ref=g_send.at[peer], dst_ref=g_recv.at[me],
            send_sem=g_send_sems.at[step], recv_sem=g_recv_sems.at[step],
            device_id={"dp": peer}, device_id_type=MESH,
        )
        copy.start()
        g_copies.append(copy)
    g_recv[me] = g_send[me]
    q_own.wait()
    q_pair.wait_recv()
    for copy in g_copies:
        copy.wait_recv()

    arrived = g_recv[...].astype(jnp.float32)
    arranged = jnp.concatenate(
        [arrived[:, m * docs:(m + 1) * docs, :].reshape(all_docs, 2 * rank) for m in range(groups)], axis=1
    ).astype(jnp.bfloat16)
    ordered = dot(place, arranged).astype(jnp.bfloat16)
    cuts, _, out_rows, width = q.shape
    scores = jnp.zeros((n * out_rows, 2 * all_docs), jnp.float32)
    for k in range(cuts):
        scores = scores + dot_nt(q[k].reshape(n * out_rows, width), ordered[:, k * width:(k + 1) * width])
    scores = scores.reshape(n, 2, out_rows // 2, 2 * all_docs)
    first_half = lax.broadcasted_iota(jnp.int32, (n, out_rows // 2, 2 * all_docs), 2) < all_docs
    s_send[...] = jnp.where(first_half, scores[:, 0], scores[:, 1])

    s_copies = []
    for step in sorted(range(1, n), key=lambda s: -abs(2 * s - n)):
        peer = lax.rem(me + step, n)
        copy = pltpu.make_async_remote_copy(
            src_ref=s_send.at[peer], dst_ref=s_recv.at[me],
            send_sem=s_send_sems.at[step], recv_sem=s_recv_sems.at[step],
            device_id={"dp": peer}, device_id_type=MESH,
        )
        copy.start()
        s_copies.append(copy)
    s_recv[me] = s_send[me]
    for copy in s_copies:
        copy.wait_recv()
    total = s_recv[0]
    for source in range(1, n):
        total = total + s_recv[source]
    half = out_rows // 2
    o_ref[0:half, :] = total[:, :all_docs]
    o_ref[half:out_rows, :] = total[:, all_docs:]
    pair_copy.wait_send()
    q_pair.wait_send()
    for copy in g_copies + s_copies:
        copy.wait_send()


def fused(activations, out_grads, counts, doc_slots, proj_in, proj_out, queries):
    n = lax.axis_size("dp")
    cuts = lax.axis_size("cuts")
    rows, rank, docs = activations.shape[0], proj_in.shape[1], counts.shape[1]
    all_docs = n * docs
    query_count, width = queries.shape
    out_rows = query_count // (n * cuts)
    block = cuts * width // LANES * docs
    chunks = (1, 1)
    anywhere = pl.BlockSpec(memory_space=pltpu.HBM)
    bf16, f32 = jnp.bfloat16, jnp.float32
    return pl.pallas_call(
        functools.partial(kernel, n, chunks),
        out_shape=pltpu.VMEM((out_rows, all_docs), f32),
        in_specs=[
            anywhere, anywhere, anywhere, anywhere, anywhere, anywhere, anywhere,
        ],
        out_specs=pl.BlockSpec(memory_space=pltpu.VMEM),
        scratch_shapes=[
            pltpu.SMEM((1, docs), jnp.int32),
            pltpu.VMEM((1, all_docs), jnp.int32),
            pltpu.VMEM(activations.shape, bf16),
            pltpu.VMEM(out_grads.shape, bf16),
            pltpu.VMEM(proj_in.shape[::-1], bf16),
            pltpu.VMEM(proj_out.shape[::-1], bf16),
            pltpu.VMEM((cuts, n, out_rows, width), bf16),
            pltpu.VMEM((rows, 2 * rank), f32),
            pltpu.VMEM((rows, 2 * rank), f32),
            pltpu.VMEM((n, block, LANES), bf16),
            pltpu.VMEM((n, block, LANES), bf16),
            pltpu.VMEM((n, out_rows // 2, 2 * all_docs), f32),
            pltpu.VMEM((n, out_rows // 2, 2 * all_docs), f32),
            pltpu.SemaphoreType.DMA((2,)),
            pltpu.SemaphoreType.DMA((2 * sum(chunks),)),
            pltpu.SemaphoreType.DMA((3,)),
            pltpu.SemaphoreType.DMA((2,)),
            pltpu.SemaphoreType.DMA((n,)),
            pltpu.SemaphoreType.DMA((n,)),
            pltpu.SemaphoreType.DMA((n,)),
            pltpu.SemaphoreType.DMA((n,)),
        ],
        compiler_params=pltpu.CompilerParams(
            collective_id=0, has_side_effects=True, vmem_limit_bytes=60 * 1024 * 1024
        ),
    )(
        counts, doc_slots.reshape(1, all_docs), activations, out_grads, proj_in.T, proj_out.T,
        queries.reshape(n, cuts, out_rows, width),
    )


def on_device(activations, out_grads, counts, doc_slots, proj_in, proj_out, queries):
    n, cuts = lax.axis_size("dp"), lax.axis_size("cuts")
    rank, docs = proj_in.shape[1], counts.shape[1]
    width = queries.shape[1]
    fits = (
        cuts == 2
        and 2 * rank == LANES
        and width % LANES == 0
        and docs % 8 == 0
        and (cuts * width // LANES * docs) % 16 == 0
        and 2 * n * docs == LANES
        and queries.shape[0] % (n * cuts * 16) == 0
        and activations.shape[0] % 16 == 0
    )
    body = fused if fits else general
    return body(activations, out_grads, counts, doc_slots, proj_in, proj_out, queries)


def solution(mesh):
    placed = (
        P(("groups", "dp"), "cuts"),
        P(("groups", "dp"), "cuts"),
        P(("groups", "dp"), None),
        P("groups"),
        P("cuts", None),
        P("cuts", None),
        P(None, ("dp", "cuts")),
    )
    return jax.shard_map(
        on_device,
        mesh=mesh,
        in_specs=placed,
        out_specs=P(("dp", "cuts"), "groups"),
        check_vma=False,
    )
```
